256 devices in a mesh: row: 32 (over y, z), col: 8 (over x, core).
Axes of the slice: x: 4, y: 4, z: 8, core: 2. Of those that a mesh axis runs over, the one named last changes fastest.
Arguments:
- krylov: bfloat16 [2048, 512], P(('row', 'col')), may hold values from -6 to 6
- jacobian_tiles: bfloat16 [49152, 128, 128], P(('row', 'col')), may hold values from -0.5 to 0.5
- tile_rows: int32 [49152], P(('row', 'col')), may hold values from 0 to 63
- tile_cols: int32 [49152], P(('row', 'col')), may hold values from 0 to 255
- live_tiles: int32 [256], P(('row', 'col')), may hold values from 1 to 192, as said below
Outputs:
- adjoint_image: float32 [2048, 512], P(('col', 'row'))
The draws below stay inside these ranges and needn't reach their ends.
Inputs may be any that keep to these rules, and one draw needn't show every extreme that they name: `live_tiles`: each device has at least one used slot; in every draw some device uses all 192 slots.
All inputs are finite; a program needn't handle non-finite values.
Results may differ from the reference program's by a relative error of at most 0.0003.
Values may be sent and summed in bfloat16 or wider, within the bound.
No kernel may reach another device: no remote copies, remote signals or barrier semaphores. Data moves between devices by JAX's collectives and lax.ppermute only.
A program may use at most 64 MiB of HBM per device.

```python
import jax
import jax.numpy as jnp
from jax import lax

TILE = 128
NVEC = 4
BLK_DEV = 8
TILE_DEV = 192
NBLK = 2048
NTILES = 49152
N_ROW = 32
N_COL = 8
DEVICES = 256


def draw_live_tiles(key, part):
    key = jax.random.fold_in(key, 7)
    lowest = max(1, TILE_DEV // 2)
    counts = jax.random.randint(key, (DEVICES,), lowest, TILE_DEV + 1)
    fullest = jax.random.randint(jax.random.fold_in(key, 1), (), 0, DEVICES)
    return jnp.where(jnp.arange(DEVICES) == fullest, TILE_DEV, counts).astype(jnp.int32)


def with_ends(result, rng, smallest, top_value):
    longest = result.shape.index(max(result.shape))
    spots = []
    for shift in (0, 1):
        where = [jax.random.randint(jax.random.fold_in(rng, axis), (), 0, length) for axis, length in enumerate(result.shape)]
        where[longest] = (where[longest] + shift) % result.shape[longest]
        spots.append(tuple(where))
    return result.at[spots[0]].set(smallest).at[spots[1]].set(top_value)


def steps_of(key, shape, shards, least, largest):
    gain = 1.0
    for dim, parts in shards:
        steps = jax.random.uniform(jax.random.fold_in(jax.random.fold_in(key, 6), dim), (parts,), jnp.float32, least / len(shards), largest / len(shards))
        gain = gain * jnp.repeat(jnp.exp(steps), shape[dim] // parts).reshape((-1,) + (1,) * (len(shape) - 1 - dim))
    return gain


def bell_draw(own_key, dims, spread, most, shards=(), held_as=jnp.bfloat16):
    level = steps_of(own_key, dims, shards, -0.22, 0.18) if shards else 1.0
    values = jax.random.normal(own_key, dims, jnp.float32) * spread * level
    return jnp.minimum(jnp.maximum(values, -most), most).astype(held_as)


def setup_inputs(seed: int = 0) -> dict:
    key_of = jax.random.split(jax.random.key(seed), 6)
    return {
        "krylov": bell_draw(key_of[0], (NBLK, NVEC * TILE), 1.0, 6.0, ((0, 256),)),
        "jacobian_tiles": bell_draw(key_of[1], (NTILES, TILE, TILE), TILE ** -0.5, 0.5, ((0, 256),)),
        "tile_rows": with_ends(jax.random.randint(key_of[2], (NTILES,), 0, N_COL * BLK_DEV), jax.random.fold_in(key_of[2], 1), 0, (N_COL * BLK_DEV) - 1).astype(jnp.int32),
        "tile_cols": with_ends(jax.random.randint(key_of[3], (NTILES,), 0, N_ROW * BLK_DEV), jax.random.fold_in(key_of[3], 1), 0, (N_ROW * BLK_DEV) - 1).astype(jnp.int32),
        "live_tiles": draw_live_tiles(jax.random.fold_in(key_of[5], 71), 0),
    }


def reference(krylov, jacobian_tiles, tile_rows, tile_cols, live_tiles):
    band_rows = N_COL * BLK_DEV
    band_cols = N_ROW * BLK_DEV
    tile_sets = jacobian_tiles.reshape(DEVICES, TILE_DEV, TILE, TILE)
    row_sets = tile_rows.reshape(DEVICES, TILE_DEV)
    col_sets = tile_cols.reshape(DEVICES, TILE_DEV)
    devices = jnp.arange(DEVICES, dtype=jnp.int32)
    slots = jnp.arange(TILE_DEV, dtype=jnp.int32)

    def accumulate(total, item):
        device, tile_set, rows_here, cols_here, used = item
        row_index = device // N_COL
        col_index = device % N_COL
        blocks = krylov[(row_index * band_rows + rows_here).astype(jnp.int32)]
        blocks = blocks.reshape(TILE_DEV, NVEC, TILE).astype(jnp.float32)
        products = jnp.einsum("tij,tvi->tvj", tile_set.astype(jnp.float32), blocks)
        kept_mask = (slots < used).astype(jnp.float32)
        products = products * kept_mask[:, None, None]
        targets = (col_index * band_cols + cols_here).astype(jnp.int32)
        total = total.at[targets].add(products.reshape(TILE_DEV, NVEC * TILE))
        return total, None

    start_total = jnp.zeros((NBLK, NVEC * TILE), jnp.float32)
    total, unused = lax.scan(accumulate, start_total, (devices, tile_sets, row_sets, col_sets, live_tiles))
    return total
```

```python
import jax
import jax.numpy as jnp
from jax import lax
from jax.sharding import PartitionSpec as P

TILE = 128


def per_device(krylov, jacobian_tiles, tile_rows, tile_cols, live_tiles):
    col_count = lax.axis_size("col")
    copies = jnp.broadcast_to(krylov[None], (col_count,) + krylov.shape)
    band_vector = lax.all_to_all(copies, "col", 0, 0).reshape(-1, krylov.shape[1])
    slot_count = jacobian_tiles.shape[0]
    row_width = krylov.shape[1]
    vector_count = row_width // TILE
    blocks = band_vector[tile_rows].reshape(slot_count, vector_count, TILE)
    products = jnp.einsum(
        "tij,tvi->tvj", jacobian_tiles, blocks, preferred_element_type=jnp.float32
    )
    kept_mask = (jnp.arange(slot_count, dtype=jnp.int32) < live_tiles[0]).astype(jnp.float32)
    weighted = (products * kept_mask[:, None, None]).reshape(slot_count, row_width)
    own_rows = krylov.shape[0]
    band_cols = lax.axis_size("row") * own_rows
    partial_sums = jax.ops.segment_sum(weighted, tile_cols, num_segments=band_cols)
    pieces = partial_sums.reshape(lax.axis_size("row"), own_rows, row_width)
    return lax.all_to_all(pieces, "row", 0, 0).sum(0)


def solution(mesh):
    placed = (
        P(("row", "col"), None),
        P(("row", "col"), None, None),
        P(("row", "col")),
        P(("row", "col")),
        P(("row", "col")),
    )
    return jax.shard_map(
        per_device, mesh=mesh, in_specs=placed, out_specs=P(("col", "row"), None), check_vma=False
    )
```

```python
import jax
import jax.numpy as jnp
from jax import lax
from jax.experimental import pallas as pl
from jax.experimental.pallas import tpu as pltpu
from jax.sharding import PartitionSpec as P

TILE = 128
SUB = 8
GROUP = 32
F32 = jnp.float32


def contribution_kernel(starts_ref, *refs):
    *band_refs, tiles_ref, out_ref, x_ref, sum_ref = refs
    vectors = band_refs[0].shape[1] // TILE
    rows = band_refs[0].shape[0]
    peers = out_ref.shape[0]
    pairs = tiles_ref.shape[0]
    x_ref[...] = jnp.zeros_like(x_ref)
    sum_ref[...] = jnp.zeros_like(sum_ref)
    for part, band_ref in enumerate(band_refs):
        for v in range(vectors):
            column = band_ref[:, v * TILE : (v + 1) * TILE].astype(F32)
            first = part * rows * SUB + v
            x_ref[0, pl.ds(first, rows, stride=SUB), :] = column
            x_ref[1, pl.ds(first + vectors, rows, stride=SUB), :] = column

    group = GROUP

    @pl.loop(0, pairs // group)
    def _(step):
        products = []
        for k in range(group):
            pair = step * group + k
            halves = []
            for half in range(2):
                start = pl.multiple_of(starts_ref[0, 2 * pair + half], SUB)
                halves.append(x_ref[half, pl.ds(start, SUB), :])
            left = jnp.concatenate(halves, axis=1).astype(jnp.bfloat16)
            products.append(jnp.dot(left, tiles_ref[pair], preferred_element_type=F32))
        for k in range(group):
            pair = step * group + k
            for half in range(2):
                start = pl.multiple_of(starts_ref[1, 2 * pair + half], SUB)
                place = pl.ds(start + half * vectors, vectors)
                sum_ref[place, :] += products[k][half * vectors : (half + 1) * vectors, :]

    lane = lax.broadcasted_iota(jnp.int32, (SUB, TILE), 1)
    own = sum_ref.shape[0] // peers

    @pl.loop(0, peers, unroll=16)
    def _(peer):
        base = pl.multiple_of(peer * own, own)
        parts = []
        exponents = jnp.zeros((SUB, TILE), F32)
        for v in range(vectors):
            first = sum_ref[pl.ds(base + v, SUB, stride=SUB), :]
            second = sum_ref[pl.ds(base + vectors + v, SUB, stride=SUB), :]
            total = first + second
            peak = jnp.max(jnp.abs(total), axis=1, keepdims=True)
            power = jnp.ceil(jnp.log2(jnp.maximum(peak, 2.0**-112)) + 0.01)
            parts.append(jnp.round(total * jnp.exp2(15.0 - power)).astype(jnp.int32))
            exponents = jnp.where(lane == v, power, exponents)
        parts.append(exponents.astype(jnp.int32))
        out_ref[peer] = jnp.concatenate(parts, axis=0).astype(jnp.int16)


def sum_kernel(in_ref, out_ref):
    peers = in_ref.shape[0]
    vectors = out_ref.shape[1] // TILE
    totals = [jnp.zeros((SUB, TILE), F32) for _ in range(vectors)]
    for peer in range(peers):
        piece = in_ref[peer].astype(jnp.int32).astype(F32)
        scale = jnp.exp2(piece[vectors * SUB :, :] - 15.0)
        for v in range(vectors):
            totals[v] += piece[v * SUB : (v + 1) * SUB, :] * scale[:, v : v + 1]
    out_ref[...] = jnp.concatenate(totals, axis=1)


def per_device(krylov, jacobian_tiles, tile_rows, tile_cols, live_tiles):
    col_count = lax.axis_size("col")
    row_count = lax.axis_size("row")
    chips = col_count // 2
    me = lax.axis_index("col")
    own_rows, row_width = krylov.shape
    slots = jacobian_tiles.shape[0]
    vectors = row_width // TILE
    other = lax.ppermute(krylov, "col", [(i, i ^ 1) for i in range(col_count)])
    own_chip = jnp.concatenate([krylov, other])
    bands = [own_chip] * chips
    for hop in (2, 1, 3):
        steps = [(i, (i + 2 * hop) % col_count) for i in range(col_count)]
        bands[hop] = lax.ppermute(own_chip, "col", steps)
    tiles = jacobian_tiles.reshape(slots // 2, 2 * TILE, TILE)
    tiles = pltpu.with_memory_space_constraint(tiles, pltpu.VMEM)
    used = jnp.arange(slots, dtype=jnp.int32) < live_tiles[0]
    holder = tile_rows // own_rows
    hops = (me // 2 - holder // 2) % chips
    place = (2 * hops + (holder + me) % 2) * own_rows + tile_rows % own_rows
    row_starts = jnp.where(used, place, own_rows * col_count) * SUB
    starts = jnp.stack([row_starts, tile_cols * SUB])
    smem = pl.BlockSpec(memory_space=pltpu.SMEM)
    vmem = pl.BlockSpec(memory_space=pltpu.VMEM)
    coded = pl.pallas_call(
        contribution_kernel,
        out_shape=jax.ShapeDtypeStruct((row_count, (vectors + 1) * SUB, TILE), jnp.int16),
        in_specs=[smem] + [vmem] * (chips + 1),
        out_specs=vmem,
        scratch_shapes=[
            pltpu.VMEM((2, (own_rows * col_count + 1) * SUB, TILE), F32),
            pltpu.VMEM((row_count * own_rows * SUB, TILE), F32),
        ],
        compiler_params=pltpu.CompilerParams(vmem_limit_bytes=24 * 2**20),
    )(starts, *bands, tiles)
    received = lax.all_to_all(coded, "row", 0, 0)
    return pl.pallas_call(
        sum_kernel,
        out_shape=jax.ShapeDtypeStruct((own_rows, row_width), F32),
        in_specs=[vmem],
        out_specs=vmem,
        compiler_params=pltpu.CompilerParams(vmem_limit_bytes=4 * 2**20),
    )(received)


def solution(mesh):
    placed = (
        P(("row", "col"), None),
        P(("row", "col"), None, None),
        P(("row", "col")),
        P(("row", "col")),
        P(("row", "col")),
    )
    return jax.shard_map(
        per_device, mesh=mesh, in_specs=placed, out_specs=P(("col", "row"), None), check_vma=False
    )
```

```python
import jax
import jax.numpy as jnp
from jax import lax
from jax.experimental import pallas as pl
from jax.experimental.pallas import tpu as pltpu
from jax.sharding import PartitionSpec as P

TILE = 128
SUB = 8
GROUP = 32
F32 = jnp.float32


def load_kernel(*refs):
    count = len(refs) // 2
    sources, targets, sems = refs[:count], refs[count : 2 * count], refs[-1]
    copies = [
        pltpu.make_async_copy(source, target, sems.at[i])
        for i, (source, target) in enumerate(zip(sources, targets))
    ]
    for copy in copies:
        copy.start()
    for copy in copies:
        copy.wait()


def contribution_kernel(live_ref, rows_ref, cols_ref, *refs):
    *band_refs, tiles_ref, out_ref, x_ref, sum_ref = refs
    vectors = band_refs[0].shape[1] // TILE
    chips = len(band_refs)
    rows = band_refs[0].shape[0] // 2
    words = vectors // 2 * SUB
    pairs = tiles_ref.shape[0]
    blocks = 2 * chips * rows
    me = lax.axis_index("col")
    live = live_ref[0]
    x_ref[...] = jnp.zeros_like(x_ref)
    sum_ref[...] = jnp.zeros_like(sum_ref)
    for hop, band_ref in enumerate(band_refs):
        chip = lax.rem(me // 2 + chips - hop, chips)
        for core in range(2):
            holder = 2 * chip + lax.rem(me + core, 2)
            base = pl.multiple_of(holder * rows * SUB, rows * SUB)
            for v in range(vectors):
                column = band_ref[core * rows : (core + 1) * rows, v * TILE : (v + 1) * TILE]
                column = column.astype(F32)
                x_ref[0, pl.ds(base + v, rows, stride=SUB), :] = column
                x_ref[1, pl.ds(base + vectors + v, rows, stride=SUB), :] = column

    @pl.loop(0, pairs // GROUP)
    def _(step):
        products = []
        for k in range(GROUP):
            pair = step * GROUP + k
            halves = []
            for half in range(2):
                slot = 2 * pair + half
                row = jnp.where(slot < live, rows_ref[slot], blocks)
                start = pl.multiple_of(row * SUB, SUB)
                halves.append(x_ref[half, pl.ds(start, SUB), :])
            left = jnp.concatenate(halves, axis=1).astype(jnp.bfloat16)
            products.append(jnp.dot(left, tiles_ref[pair], preferred_element_type=F32))
        for k in range(GROUP):
            pair = step * GROUP + k
            for half in range(2):
                start = pl.multiple_of(cols_ref[2 * pair + half] * SUB, SUB)
                place = pl.ds(start + half * vectors, vectors)
                sum_ref[place, :] += products[k][half * vectors : (half + 1) * vectors, :]

    lane = lax.broadcasted_iota(jnp.int32, (SUB, TILE), 1)
    sub = lax.broadcasted_iota(jnp.int32, (SUB, TILE), 0)
    peers = out_ref.shape[0] // (words + 1)
    own = sum_ref.shape[0] // peers
    for peer in range(peers):
        base, first_row = peer * own, peer * (words + 1)
        codes = []
        powers = jnp.zeros((SUB, TILE), F32)
        for v in range(vectors):
            first = sum_ref[pl.ds(base + v, SUB, stride=SUB), :]
            second = sum_ref[pl.ds(base + vectors + v, SUB, stride=SUB), :]
            total = first + second
            peak = jnp.max(jnp.abs(total), axis=1, keepdims=True)
            power = jnp.ceil(jnp.log2(jnp.maximum(peak, 2.0**-111)) + 0.01)
            codes.append(jnp.round(total * jnp.exp2(15.0 - power)).astype(jnp.int32))
            powers = jnp.where(lane == sub * vectors + v, power, powers)
        for half in range(vectors // 2):
            word = (codes[2 * half] << 16) | (codes[2 * half + 1] & 0xFFFF)
            out_ref[first_row + half * SUB : first_row + (half + 1) * SUB, :] = word
        row = jnp.sum(powers, axis=0, keepdims=True).astype(jnp.int32)
        out_ref[first_row + words : first_row + words + 1, :] = row


def sum_kernel(in_ref, out_ref):
    vectors = out_ref.shape[1] // TILE
    words = vectors // 2 * SUB
    peers = in_ref.shape[0] // (words + 1)
    lane = lax.broadcasted_iota(jnp.int32, (SUB, TILE), 1)
    sub = lax.broadcasted_iota(jnp.int32, (SUB, TILE), 0)
    totals = [jnp.zeros((SUB, TILE), F32) for _ in range(vectors)]
    for peer in range(peers):
        first_row = peer * (words + 1)
        row = in_ref[first_row + words : first_row + words + 1, :]
        scales = jnp.broadcast_to(jnp.exp2(row.astype(F32) - 15.0), (SUB, TILE))
        for half in range(vectors // 2):
            word = in_ref[first_row + half * SUB : first_row + (half + 1) * SUB, :]
            for v, code in ((2 * half, word >> 16), (2 * half + 1, (word << 16) >> 16)):
                picked = jnp.where(lane == sub * vectors + v, scales, 0.0)
                totals[v] += code.astype(F32) * jnp.sum(picked, axis=1, keepdims=True)
    out_ref[...] = jnp.concatenate(totals, axis=1)


def per_device(krylov, jacobian_tiles, tile_rows, tile_cols, live_tiles):
    col_count = lax.axis_size("col")
    row_count = lax.axis_size("row")
    chips = col_count // 2
    own_rows, row_width = krylov.shape
    slots = jacobian_tiles.shape[0]
    vectors = row_width // TILE
    words = vectors // 2 * SUB
    smem = pl.BlockSpec(memory_space=pltpu.SMEM)
    vmem = pl.BlockSpec(memory_space=pltpu.VMEM)

    other = lax.ppermute(krylov, "col", [(i, i ^ 1) for i in range(col_count)])
    own_chip = jnp.concatenate([krylov, other])
    bands = [own_chip] * chips
    for hop in (2, 1, 3):
        steps = [(i, (i + 2 * hop) % col_count) for i in range(col_count)]
        bands[hop] = lax.ppermute(own_chip, "col", steps)

    held = [jacobian_tiles.reshape(slots // 2, 2 * TILE, TILE)]
    held = [pltpu.with_memory_space_constraint(a, pltpu.HBM) for a in held]
    (tiles,) = pl.pallas_call(
        load_kernel,
        out_shape=[pltpu.VMEM(a.shape, a.dtype) for a in held],
        in_specs=[pl.BlockSpec(memory_space=pltpu.HBM)] * len(held),
        out_specs=[vmem] * len(held),
        scratch_shapes=[pltpu.SemaphoreType.DMA((len(held),))],
        compiler_params=pltpu.CompilerParams(vmem_limit_bytes=2**20),
        cost_estimate=pl.CostEstimate(flops=0, bytes_accessed=4 * jacobian_tiles.size, transcendentals=0),
    )(*held)
    tiles = pltpu.with_memory_space_constraint(tiles, pltpu.VMEM)
    coded = pl.pallas_call(
        contribution_kernel,
        out_shape=jax.ShapeDtypeStruct((row_count * (words + 1), TILE), jnp.int32),
        in_specs=[smem, smem, smem] + [vmem] * (chips + 1),
        out_specs=vmem,
        scratch_shapes=[
            pltpu.VMEM((2, (own_rows * col_count + 1) * SUB, TILE), F32),
            pltpu.VMEM((row_count * own_rows * SUB, TILE), F32),
        ],
        compiler_params=pltpu.CompilerParams(vmem_limit_bytes=24 * 2**20),
    )(live_tiles, tile_rows, tile_cols, *bands, tiles)
    pieces = coded.reshape(row_count, words + 1, 1, TILE)
    received = lax.all_to_all(pieces, "row", 0, 0).reshape(coded.shape)
    return pl.pallas_call(
        sum_kernel,
        out_shape=jax.ShapeDtypeStruct((own_rows, row_width), F32),
        in_specs=[vmem],
        out_specs=vmem,
        compiler_params=pltpu.CompilerParams(vmem_limit_bytes=4 * 2**20),
    )(received)


def solution(mesh):
    placed = (
        P(("row", "col"), None),
        P(("row", "col"), None, None),
        P(("row", "col")),
        P(("row", "col")),
        P(("row", "col")),
    )
    return jax.shard_map(
        per_device, mesh=mesh, in_specs=placed, out_specs=P(("col", "row"), None), check_vma=False
    )
```

```python
import jax
import jax.numpy as jnp
from jax import lax
from jax.experimental import pallas as pl
from jax.experimental.pallas import tpu as pltpu
from jax.sharding import PartitionSpec as P

TILE = 128
SUB = 8
GROUP = 32
HOPS = (1, 2, 3)
F32 = jnp.float32


def join_kernel(*refs):
    *part_refs, tiles_ref, out_ref = refs
    for i, part_ref in enumerate(part_refs):
        out_ref[i] = part_ref[...]


def contribution_kernel(live_ref, rows_ref, cols_ref, *refs):
    pair_ref, joined_ref, tiles_ref, out_ref, x_ref, sum_ref = refs
    rows, row_width = pair_ref.shape[0] // 2, pair_ref.shape[1]
    vectors = row_width // TILE
    chips = joined_ref.shape[0] + 1
    words = vectors // 2 * SUB
    pairs = tiles_ref.shape[0]
    blocks = 2 * chips * rows
    me = lax.axis_index("col")
    live = live_ref[0]
    x_ref[...] = jnp.zeros_like(x_ref)
    sum_ref[...] = jnp.zeros_like(sum_ref)
    for hop in range(chips):
        chip = (me // 2) ^ hop
        for part in range(2):
            holder = 2 * chip + lax.rem(me + part, 2)
            base = pl.multiple_of(holder * rows * SUB, rows * SUB)
            for v in range(vectors):
                window = (pl.ds(part * rows, rows), pl.ds(v * TILE, TILE))
                column = pair_ref[window] if hop == 0 else joined_ref[(hop - 1, *window)]
                column = column.astype(F32)
                x_ref[0, pl.ds(base + v, rows, stride=SUB), :] = column
                x_ref[1, pl.ds(base + vectors + v, rows, stride=SUB), :] = column

    @pl.loop(0, pairs // GROUP)
    def _(step):
        products = []
        for k in range(GROUP):
            pair = step * GROUP + k
            halves = []
            for half in range(2):
                slot = 2 * pair + half
                row = jnp.where(slot < live, rows_ref[slot], blocks)
                start = pl.multiple_of(row * SUB, SUB)
                halves.append(x_ref[half, pl.ds(start, SUB), :])
            left = jnp.concatenate(halves, axis=1).astype(jnp.bfloat16)
            products.append(jnp.dot(left, tiles_ref[pair], preferred_element_type=F32))
        for k in range(GROUP):
            pair = step * GROUP + k
            for half in range(2):
                start = pl.multiple_of(cols_ref[2 * pair + half] * SUB, SUB)
                place = pl.ds(start + half * vectors, vectors)
                sum_ref[place, :] += products[k][half * vectors : (half + 1) * vectors, :]

    lane = lax.broadcasted_iota(jnp.int32, (SUB, TILE), 1)
    sub = lax.broadcasted_iota(jnp.int32, (SUB, TILE), 0)
    peers = out_ref.shape[0] // (words + 1)
    own = sum_ref.shape[0] // peers
    for peer in range(peers):
        base, first_row = peer * own, peer * (words + 1)
        codes = []
        powers = jnp.zeros((SUB, TILE), F32)
        for v in range(vectors):
            first = sum_ref[pl.ds(base + v, SUB, stride=SUB), :]
            second = sum_ref[pl.ds(base + vectors + v, SUB, stride=SUB), :]
            total = first + second
            peak = jnp.max(jnp.abs(total), axis=1, keepdims=True)
            power = jnp.ceil(jnp.log2(jnp.maximum(peak, 2.0**-111)) + 0.01)
            codes.append(jnp.round(total * jnp.exp2(15.0 - power)).astype(jnp.int32))
            powers = jnp.where(lane == sub * vectors + v, power, powers)
        for half in range(vectors // 2):
            word = (codes[2 * half] << 16) | (codes[2 * half + 1] & 0xFFFF)
            out_ref[first_row + half * SUB : first_row + (half + 1) * SUB, :] = word
        row = jnp.sum(powers, axis=0, keepdims=True).astype(jnp.int32)
        out_ref[first_row + words : first_row + words + 1, :] = row


def sum_kernel(in_ref, out_ref):
    vectors = out_ref.shape[1] // TILE
    words = vectors // 2 * SUB
    peers = in_ref.shape[0] // (words + 1)
    lane = lax.broadcasted_iota(jnp.int32, (SUB, TILE), 1)
    sub = lax.broadcasted_iota(jnp.int32, (SUB, TILE), 0)
    totals = [jnp.zeros((SUB, TILE), F32) for _ in range(vectors)]
    for peer in range(peers):
        first_row = peer * (words + 1)
        row = in_ref[first_row + words : first_row + words + 1, :]
        scales = jnp.broadcast_to(jnp.exp2(row.astype(F32) - 15.0), (SUB, TILE))
        for half in range(vectors // 2):
            word = in_ref[first_row + half * SUB : first_row + (half + 1) * SUB, :]
            for v, code in ((2 * half, word >> 16), (2 * half + 1, (word << 16) >> 16)):
                picked = jnp.where(lane == sub * vectors + v, scales, 0.0)
                totals[v] += code.astype(F32) * jnp.sum(picked, axis=1, keepdims=True)
    out_ref[...] = jnp.concatenate(totals, axis=1)


def per_device(krylov, jacobian_tiles, tile_rows, tile_cols, live_tiles):
    col_count = lax.axis_size("col")
    row_count = lax.axis_size("row")
    chips = col_count // 2
    own_rows, row_width = krylov.shape
    slots = jacobian_tiles.shape[0]
    vectors = row_width // TILE
    words = vectors // 2 * SUB
    smem = pl.BlockSpec(memory_space=pltpu.SMEM)
    vmem = pl.BlockSpec(memory_space=pltpu.VMEM)

    other = lax.ppermute(krylov, "col", [(i, i ^ 1) for i in range(col_count)])
    pair = jnp.concatenate([krylov, other])
    far = [None] * chips
    for hop in HOPS:
        steps = [(i, i ^ (2 * hop)) for i in range(col_count)]
        far[hop] = lax.ppermute(pair, "col", steps)
    tiles = jacobian_tiles.reshape(slots // 2, 2 * TILE, TILE)
    joined = pl.pallas_call(
        join_kernel,
        out_shape=jax.ShapeDtypeStruct((chips - 1, 2 * own_rows, row_width), krylov.dtype),
        in_specs=[vmem] * (chips - 1) + [pl.BlockSpec(memory_space=pltpu.HBM)],
        out_specs=vmem,
        compiler_params=pltpu.CompilerParams(vmem_limit_bytes=2**20),
        cost_estimate=pl.CostEstimate(flops=0, bytes_accessed=4 * jacobian_tiles.size, transcendentals=0),
    )(*far[1:], pltpu.with_memory_space_constraint(tiles, pltpu.HBM))
    coded = pl.pallas_call(
        contribution_kernel,
        out_shape=jax.ShapeDtypeStruct((row_count * (words + 1), TILE), jnp.int32),
        in_specs=[smem, smem, smem] + [vmem] * 3,
        out_specs=vmem,
        scratch_shapes=[
            pltpu.VMEM((2, (own_rows * col_count + 1) * SUB, TILE), F32),
            pltpu.VMEM((row_count * own_rows * SUB, TILE), F32),
        ],
        compiler_params=pltpu.CompilerParams(vmem_limit_bytes=10 * 2**20),
    )(live_tiles, tile_rows, tile_cols, pair, joined, tiles)
    pieces = coded.reshape(row_count, words + 1, 1, TILE)
    received = lax.all_to_all(pieces, "row", 0, 0).reshape(coded.shape)
    return pl.pallas_call(
        sum_kernel,
        out_shape=jax.ShapeDtypeStruct((own_rows, row_width), F32),
        in_specs=[vmem],
        out_specs=vmem,
        compiler_params=pltpu.CompilerParams(vmem_limit_bytes=4 * 2**20),
    )(received)


def solution(mesh):
    placed = (
        P(("row", "col"), None),
        P(("row", "col"), None, None),
        P(("row", "col")),
        P(("row", "col")),
        P(("row", "col")),
    )
    return jax.shard_map(
        per_device, mesh=mesh, in_specs=placed, out_specs=P(("col", "row"), None), check_vma=False
    )
```

```python
import jax
import jax.numpy as jnp
from jax import lax
from jax.experimental import pallas as pl
from jax.experimental.pallas import tpu as pltpu
from jax.sharding import PartitionSpec as P

TILE = 128
SUB = 8
GROUP = 48
HOPS = (1, 2, 3)
F32 = jnp.float32


def join_kernel(*refs):
    *part_refs, tiles_ref, out_ref = refs
    for i, part_ref in enumerate(part_refs):
        out_ref[i] = part_ref[...]


def contribution_kernel(live_ref, *refs):
    index_refs, refs = refs[:2], refs[2:]
    pair_ref, joined_ref, tiles_ref, out_ref, x_ref, sum_ref, rows_ref, cols_ref, sems = refs
    copies = [
        pltpu.make_async_copy(source, target, sems.at[i])
        for i, (source, target) in enumerate(zip(index_refs, (rows_ref, cols_ref)))
    ]
    for copy in copies:
        copy.start()
    rows, row_width = pair_ref.shape[0] // 2, pair_ref.shape[1]
    vectors = row_width // TILE
    chips = joined_ref.shape[0] + 1
    words = vectors // 2 * SUB
    pairs = tiles_ref.shape[0]
    blocks = 2 * chips * rows
    me = lax.axis_index("col")
    live = live_ref[0]
    x_ref[...] = jnp.zeros_like(x_ref)
    sum_ref[...] = jnp.zeros_like(sum_ref)
    for hop in range(chips):
        chip = (me // 2) ^ hop
        for part in range(2):
            holder = 2 * chip + lax.rem(me + part, 2)
            base = pl.multiple_of(holder * rows * SUB, rows * SUB)
            for v in range(vectors):
                window = (pl.ds(part * rows, rows), pl.ds(v * TILE, TILE))
                column = pair_ref[window] if hop == 0 else joined_ref[(hop - 1, *window)]
                column = column.astype(F32)
                x_ref[0, pl.ds(base + v, rows, stride=SUB), :] = column
                x_ref[1, pl.ds(base + vectors + v, rows, stride=SUB), :] = column

    for copy in copies:
        copy.wait()

    for step in range(pairs // GROUP):
        products = []
        for k in range(GROUP):
            pair = step * GROUP + k
            halves = []
            for half in range(2):
                slot = 2 * pair + half
                row = jnp.where(slot < live, rows_ref[slot], blocks)
                start = pl.multiple_of(row * SUB, SUB)
                halves.append(x_ref[half, pl.ds(start, SUB), :])
            left = jnp.concatenate(halves, axis=1).astype(jnp.bfloat16)
            products.append(jnp.dot(left, tiles_ref[pair], preferred_element_type=F32))
        for k in range(GROUP):
            pair = step * GROUP + k
            for half in range(2):
                start = pl.multiple_of(cols_ref[2 * pair + half] * SUB, SUB)
                place = pl.ds(start + half * vectors, vectors)
                sum_ref[place, :] += products[k][half * vectors : (half + 1) * vectors, :]

    lane = lax.broadcasted_iota(jnp.int32, (SUB, TILE), 1)
    sub = lax.broadcasted_iota(jnp.int32, (SUB, TILE), 0)
    peers = out_ref.shape[0] // (words + 1)
    own = sum_ref.shape[0] // peers
    for peer in range(peers):
        base, first_row = peer * own, peer * (words + 1)
        codes = []
        powers = jnp.zeros((SUB, TILE), F32)
        for v in range(vectors):
            first = sum_ref[pl.ds(base + v, SUB, stride=SUB), :]
            second = sum_ref[pl.ds(base + vectors + v, SUB, stride=SUB), :]
            total = first + second
            peak = jnp.max(jnp.abs(total), axis=1, keepdims=True)
            power = jnp.ceil(jnp.log2(jnp.maximum(peak, 2.0**-111)) + 0.01)
            codes.append(jnp.round(total * jnp.exp2(15.0 - power)).astype(jnp.int32))
            powers = jnp.where(lane == sub * vectors + v, power, powers)
        for half in range(vectors // 2):
            word = (codes[2 * half] << 16) | (codes[2 * half + 1] & 0xFFFF)
            out_ref[first_row + half * SUB : first_row + (half + 1) * SUB, :] = word
        row = jnp.sum(powers, axis=0, keepdims=True).astype(jnp.int32)
        out_ref[first_row + words : first_row + words + 1, :] = row


def sum_kernel(in_ref, out_ref):
    vectors = out_ref.shape[1] // TILE
    words = vectors // 2 * SUB
    peers = in_ref.shape[0] // (words + 1)
    lane = lax.broadcasted_iota(jnp.int32, (SUB, TILE), 1)
    sub = lax.broadcasted_iota(jnp.int32, (SUB, TILE), 0)
    totals = [jnp.zeros((SUB, TILE), F32) for _ in range(vectors)]
    for peer in range(peers):
        first_row = peer * (words + 1)
        row = in_ref[first_row + words : first_row + words + 1, :]
        scales = jnp.broadcast_to(jnp.exp2(row.astype(F32) - 15.0), (SUB, TILE))
        for half in range(vectors // 2):
            word = in_ref[first_row + half * SUB : first_row + (half + 1) * SUB, :]
            for v, code in ((2 * half, word >> 16), (2 * half + 1, (word << 16) >> 16)):
                picked = jnp.where(lane == sub * vectors + v, scales, 0.0)
                totals[v] += code.astype(F32) * jnp.sum(picked, axis=1, keepdims=True)
    out_ref[...] = jnp.concatenate(totals, axis=1)


def per_device(krylov, jacobian_tiles, tile_rows, tile_cols, live_tiles):
    col_count = lax.axis_size("col")
    row_count = lax.axis_size("row")
    chips = col_count // 2
    own_rows, row_width = krylov.shape
    slots = jacobian_tiles.shape[0]
    vectors = row_width // TILE
    words = vectors // 2 * SUB
    smem = pl.BlockSpec(memory_space=pltpu.SMEM)
    vmem = pl.BlockSpec(memory_space=pltpu.VMEM)

    other = lax.ppermute(krylov, "col", [(i, i ^ 1) for i in range(col_count)])
    pair = jnp.concatenate([krylov, other])
    far = [None] * chips
    for hop in HOPS:
        steps = [(i, i ^ (2 * hop)) for i in range(col_count)]
        far[hop] = lax.ppermute(pair, "col", steps)
    tiles = jacobian_tiles.reshape(slots // 2, 2 * TILE, TILE)
    joined = pl.pallas_call(
        join_kernel,
        out_shape=jax.ShapeDtypeStruct((chips - 1, 2 * own_rows, row_width), krylov.dtype),
        in_specs=[vmem] * (chips - 1) + [pl.BlockSpec(memory_space=pltpu.HBM)],
        out_specs=vmem,
        compiler_params=pltpu.CompilerParams(vmem_limit_bytes=2**20),
        cost_estimate=pl.CostEstimate(flops=0, bytes_accessed=4 * jacobian_tiles.size, transcendentals=0),
    )(*far[1:], pltpu.with_memory_space_constraint(tiles, pltpu.HBM))
    coded = pl.pallas_call(
        contribution_kernel,
        out_shape=jax.ShapeDtypeStruct((row_count * (words + 1), TILE), jnp.int32),
        in_specs=[smem] + [vmem] * 5,
        out_specs=vmem,
        scratch_shapes=[
            pltpu.VMEM((2, (own_rows * col_count + 1) * SUB, TILE), F32),
            pltpu.VMEM((row_count * own_rows * SUB, TILE), F32),
            pltpu.SMEM(tile_rows.shape, tile_rows.dtype),
            pltpu.SMEM(tile_cols.shape, tile_cols.dtype),
            pltpu.SemaphoreType.DMA((2,)),
        ],
        compiler_params=pltpu.CompilerParams(vmem_limit_bytes=10 * 2**20),
    )(live_tiles, tile_rows, tile_cols, pair, joined, tiles)
    pieces = coded.reshape(row_count, words + 1, 1, TILE)
    received = lax.all_to_all(pieces, "row", 0, 0).reshape(coded.shape)
    return pl.pallas_call(
        sum_kernel,
        out_shape=jax.ShapeDtypeStruct((own_rows, row_width), F32),
        in_specs=[vmem],
        out_specs=vmem,
        compiler_params=pltpu.CompilerParams(vmem_limit_bytes=4 * 2**20),
    )(received)


def solution(mesh):
    placed = (
        P(("row", "col"), None),
        P(("row", "col"), None, None),
        P(("row", "col")),
        P(("row", "col")),
        P(("row", "col")),
    )
    return jax.shard_map(
        per_device, mesh=mesh, in_specs=placed, out_specs=P(("col", "row"), None), check_vma=False
    )
```

```python
import functools

import jax
import jax.numpy as jnp
from jax import lax
from jax.experimental import pallas as pl
from jax.experimental.pallas import tpu as pltpu
from jax.sharding import PartitionSpec as P

TILE = 128
SUB = 8
GROUP = 48
HOPS = (1, 2, 3)
F32 = jnp.float32


def join_kernel(*refs):
    *part_refs, tiles_ref, out_ref = refs
    for i, part_ref in enumerate(part_refs):
        out_ref[i] = part_ref[...]


def contribution_kernel(live_ref, *refs):
    index_refs, refs = refs[:2], refs[2:]
    pair_ref, joined_ref, tiles_ref, out_ref, x_ref, sum_ref, rows_ref, cols_ref, sems = refs
    copies = [
        pltpu.make_async_copy(source, target, sems.at[i])
        for i, (source, target) in enumerate(zip(index_refs, (rows_ref, cols_ref)))
    ]
    for copy in copies:
        copy.start()
    rows, row_width = pair_ref.shape[0] // 2, pair_ref.shape[1]
    vectors = row_width // TILE
    chips = joined_ref.shape[0] + 1
    words = vectors // 2 * SUB
    pairs = tiles_ref.shape[0]
    blocks = 2 * chips * rows
    me = lax.axis_index("col")
    live = live_ref[0]
    x_ref[...] = jnp.zeros_like(x_ref)
    sum_ref[...] = jnp.zeros_like(sum_ref)
    for hop in range(chips):
        chip = (me // 2) ^ hop
        for part in range(2):
            holder = 2 * chip + lax.rem(me + part, 2)
            base = pl.multiple_of(holder * rows * SUB, rows * SUB)
            for v in range(vectors):
                window = (pl.ds(part * rows, rows), pl.ds(v * TILE, TILE))
                column = pair_ref[window] if hop == 0 else joined_ref[(hop - 1, *window)]
                column = column.astype(F32)
                x_ref[0, pl.ds(base + v, rows, stride=SUB), :] = column
                x_ref[1, pl.ds(base + vectors + v, rows, stride=SUB), :] = column

    for copy in copies:
        copy.wait()

    for step in range(pairs // GROUP):
        products = []
        for k in range(GROUP):
            pair = step * GROUP + k
            halves = []
            for half in range(2):
                slot = 2 * pair + half
                row = jnp.where(slot < live, rows_ref[slot], blocks)
                start = pl.multiple_of(row * SUB, SUB)
                halves.append(x_ref[half, pl.ds(start, SUB), :])
            left = jnp.concatenate(halves, axis=1).astype(jnp.bfloat16)
            products.append(jnp.dot(left, tiles_ref[pair], preferred_element_type=F32))
        for k in range(GROUP):
            pair = step * GROUP + k
            for half in range(2):
                start = pl.multiple_of(cols_ref[2 * pair + half] * SUB, SUB)
                place = pl.ds(start + half * vectors, vectors)
                sum_ref[place, :] += products[k][half * vectors : (half + 1) * vectors, :]

    peers = out_ref.shape[0] // (words + 1)
    own = sum_ref.shape[0] // peers
    for peer in range(peers):
        base, first_row = peer * own, peer * (words + 1)
        totals = []
        for v in range(vectors):
            first = sum_ref[pl.ds(base + v, SUB, stride=SUB), :]
            second = sum_ref[pl.ds(base + vectors + v, SUB, stride=SUB), :]
            totals.append(first + second)
        peaks = functools.reduce(jnp.maximum, [jnp.abs(total) for total in totals])
        peak = jnp.max(peaks, axis=0, keepdims=True)
        power = jnp.ceil(jnp.log2(jnp.maximum(peak, 2.0**-111)) + 0.01)
        scale = jnp.exp2(15.0 - power)
        codes = [jnp.round(total * scale).astype(jnp.int32) for total in totals]
        for half in range(vectors // 2):
            word = (codes[2 * half] << 16) | (codes[2 * half + 1] & 0xFFFF)
            out_ref[first_row + half * SUB : first_row + (half + 1) * SUB, :] = word
        out_ref[first_row + words : first_row + words + 1, :] = power.astype(jnp.int32)


def sum_kernel(in_ref, out_ref):
    vectors = out_ref.shape[1] // TILE
    words = vectors // 2 * SUB
    peers = in_ref.shape[0] // (words + 1)
    totals = [jnp.zeros((SUB, TILE), F32) for _ in range(vectors)]
    for peer in range(peers):
        first_row = peer * (words + 1)
        row = in_ref[first_row + words : first_row + words + 1, :]
        scale = jnp.exp2(row.astype(F32) - 15.0)
        for half in range(vectors // 2):
            word = in_ref[first_row + half * SUB : first_row + (half + 1) * SUB, :]
            totals[2 * half] += (word >> 16).astype(F32) * scale
            totals[2 * half + 1] += ((word << 16) >> 16).astype(F32) * scale
    out_ref[...] = jnp.concatenate(totals, axis=1)


def per_device(krylov, jacobian_tiles, tile_rows, tile_cols, live_tiles):
    col_count = lax.axis_size("col")
    row_count = lax.axis_size("row")
    chips = col_count // 2
    own_rows, row_width = krylov.shape
    slots = jacobian_tiles.shape[0]
    vectors = row_width // TILE
    words = vectors // 2 * SUB
    smem = pl.BlockSpec(memory_space=pltpu.SMEM)
    vmem = pl.BlockSpec(memory_space=pltpu.VMEM)

    other = lax.ppermute(krylov, "col", [(i, i ^ 1) for i in range(col_count)])
    pair = jnp.concatenate([krylov, other])
    far = [None] * chips
    for hop in HOPS:
        steps = [(i, i ^ (2 * hop)) for i in range(col_count)]
        far[hop] = lax.ppermute(pair, "col", steps)
    tiles = jacobian_tiles.reshape(slots // 2, 2 * TILE, TILE)
    joined = pl.pallas_call(
        join_kernel,
        out_shape=jax.ShapeDtypeStruct((chips - 1, 2 * own_rows, row_width), krylov.dtype),
        in_specs=[vmem] * (chips - 1) + [pl.BlockSpec(memory_space=pltpu.HBM)],
        out_specs=vmem,
        compiler_params=pltpu.CompilerParams(vmem_limit_bytes=2**20),
        cost_estimate=pl.CostEstimate(flops=0, bytes_accessed=4 * jacobian_tiles.size, transcendentals=0),
    )(*far[1:], pltpu.with_memory_space_constraint(tiles, pltpu.HBM))
    coded = pl.pallas_call(
        contribution_kernel,
        out_shape=jax.ShapeDtypeStruct((row_count * (words + 1), TILE), jnp.int32),
        in_specs=[smem] + [vmem] * 5,
        out_specs=vmem,
        scratch_shapes=[
            pltpu.VMEM((2, (own_rows * col_count + 1) * SUB, TILE), F32),
            pltpu.VMEM((row_count * own_rows * SUB, TILE), F32),
            pltpu.SMEM(tile_rows.shape, tile_rows.dtype),
            pltpu.SMEM(tile_cols.shape, tile_cols.dtype),
            pltpu.SemaphoreType.DMA((2,)),
        ],
        compiler_params=pltpu.CompilerParams(vmem_limit_bytes=10 * 2**20),
    )(live_tiles, tile_rows, tile_cols, pair, joined, tiles)
    pieces = coded.reshape(row_count, words + 1, 1, TILE)
    received = lax.all_to_all(pieces, "row", 0, 0).reshape(coded.shape)
    return pl.pallas_call(
        sum_kernel,
        out_shape=jax.ShapeDtypeStruct((own_rows, row_width), F32),
        in_specs=[vmem],
        out_specs=vmem,
        compiler_params=pltpu.CompilerParams(vmem_limit_bytes=4 * 2**20),
    )(received)


def solution(mesh):
    placed = (
        P(("row", "col"), None),
        P(("row", "col"), None, None),
        P(("row", "col")),
        P(("row", "col")),
        P(("row", "col")),
    )
    return jax.shard_map(
        per_device, mesh=mesh, in_specs=placed, out_specs=P(("col", "row"), None), check_vma=False
    )
```

```python
import functools

import jax
import jax.numpy as jnp
from jax import lax
from jax.experimental import pallas as pl
from jax.experimental.pallas import tpu as pltpu
from jax.sharding import PartitionSpec as P

TILE = 128
SUB = 8
GROUP = 48
PEERS = [4, 12, 24, 2, 28, 10, 18, 27, 21, 9, 19, 8, 6, 17, 13, 15, 29, 3, 5, 1, 7, 14, 0, 31, 20, 30, 26, 22, 25, 11, 23, 16]
HOPS = (1, 2, 3)
F32 = jnp.float32


def join_kernel(*refs):
    *part_refs, tiles_ref, out_ref = refs
    for i, part_ref in enumerate(part_refs):
        out_ref[i] = part_ref[...]


def contribution_kernel(live_ref, *refs):
    index_refs, refs = refs[:2], refs[2:]
    pair_ref, joined_ref, tiles_ref, out_ref, x_ref, sum_ref, rows_ref, cols_ref, sems = refs
    copies = [
        pltpu.make_async_copy(source, target, sems.at[i])
        for i, (source, target) in enumerate(zip(index_refs, (rows_ref, cols_ref)))
    ]
    for copy in copies:
        copy.start()
    rows, row_width = pair_ref.shape[0] // 2, pair_ref.shape[1]
    vectors = row_width // TILE
    chips = joined_ref.shape[0] + 1
    words = vectors // 2 * SUB
    pairs = tiles_ref.shape[0]
    blocks = 2 * chips * rows
    me = lax.axis_index("col")
    live = live_ref[0]
    x_ref[...] = jnp.zeros_like(x_ref)
    sum_ref[...] = jnp.zeros_like(sum_ref)
    for hop in range(chips):
        chip = (me // 2) ^ hop
        for part in range(2):
            holder = 2 * chip + lax.rem(me + part, 2)
            base = pl.multiple_of(holder * rows * SUB, rows * SUB)
            for v in range(vectors):
                window = (pl.ds(part * rows, rows), pl.ds(v * TILE, TILE))
                column = pair_ref[window] if hop == 0 else joined_ref[(hop - 1, *window)]
                column = column.astype(F32)
                x_ref[0, pl.ds(base + v, rows, stride=SUB), :] = column
                x_ref[1, pl.ds(base + vectors + v, rows, stride=SUB), :] = column

    for copy in copies:
        copy.wait()

    for step in range(pairs // GROUP):
        products = []
        for k in range(GROUP):
            pair = step * GROUP + k
            halves = []
            for half in range(2):
                slot = 2 * pair + half
                row = jnp.where(slot < live, rows_ref[slot], blocks)
                start = pl.multiple_of(row * SUB, SUB)
                halves.append(x_ref[half, pl.ds(start, SUB), :])
            left = jnp.concatenate(halves, axis=1).astype(jnp.bfloat16)
            products.append(jnp.dot(left, tiles_ref[pair], preferred_element_type=F32))
        for k in range(GROUP):
            pair = step * GROUP + k
            for half in range(2):
                start = pl.multiple_of(cols_ref[2 * pair + half] * SUB, SUB)
                place = pl.ds(start + half * vectors, vectors)
                sum_ref[place, :] += products[k][half * vectors : (half + 1) * vectors, :]

    peers = out_ref.shape[0] // (words + 1)
    own = sum_ref.shape[0] // peers
    for peer in range(peers):
        base, first_row = PEERS[peer] * own, peer * (words + 1)
        totals = []
        for v in range(vectors):
            first = sum_ref[pl.ds(base + v, SUB, stride=SUB), :]
            second = sum_ref[pl.ds(base + vectors + v, SUB, stride=SUB), :]
            totals.append(first + second)
        peaks = functools.reduce(jnp.maximum, [jnp.abs(total) for total in totals])
        peak = jnp.max(peaks, axis=0, keepdims=True)
        power = jnp.ceil(jnp.log2(jnp.maximum(peak, 2.0**-111)) + 0.01)
        scale = jnp.exp2(15.0 - power)
        codes = [jnp.round(total * scale).astype(jnp.int32) for total in totals]
        for half in range(vectors // 2):
            word = (codes[2 * half] << 16) | (codes[2 * half + 1] & 0xFFFF)
            out_ref[first_row + half * SUB : first_row + (half + 1) * SUB, :] = word
        out_ref[first_row + words : first_row + words + 1, :] = power.astype(jnp.int32)


def sum_kernel(in_ref, out_ref):
    vectors = out_ref.shape[1] // TILE
    words = vectors // 2 * SUB
    peers = in_ref.shape[0] // (words + 1)
    totals = [jnp.zeros((SUB, TILE), F32) for _ in range(vectors)]
    for peer in range(peers):
        first_row = peer * (words + 1)
        row = in_ref[first_row + words : first_row + words + 1, :]
        scale = jnp.exp2(row.astype(F32) - 15.0)
        for half in range(vectors // 2):
            word = in_ref[first_row + half * SUB : first_row + (half + 1) * SUB, :]
            totals[2 * half] += (word >> 16).astype(F32) * scale
            totals[2 * half + 1] += ((word << 16) >> 16).astype(F32) * scale
    out_ref[...] = jnp.concatenate(totals, axis=1)


def per_device(krylov, jacobian_tiles, tile_rows, tile_cols, live_tiles):
    col_count = lax.axis_size("col")
    row_count = lax.axis_size("row")
    chips = col_count // 2
    own_rows, row_width = krylov.shape
    slots = jacobian_tiles.shape[0]
    vectors = row_width // TILE
    words = vectors // 2 * SUB
    smem = pl.BlockSpec(memory_space=pltpu.SMEM)
    vmem = pl.BlockSpec(memory_space=pltpu.VMEM)

    other = lax.ppermute(krylov, "col", [(i, i ^ 1) for i in range(col_count)])
    pair = jnp.concatenate([krylov, other])
    far = [None] * chips
    for hop in HOPS:
        steps = [(i, i ^ (2 * hop)) for i in range(col_count)]
        far[hop] = lax.ppermute(pair, "col", steps)
    tiles = jacobian_tiles.reshape(slots // 2, 2 * TILE, TILE)
    joined = pl.pallas_call(
        join_kernel,
        out_shape=jax.ShapeDtypeStruct((chips - 1, 2 * own_rows, row_width), krylov.dtype),
        in_specs=[vmem] * (chips - 1) + [pl.BlockSpec(memory_space=pltpu.HBM)],
        out_specs=vmem,
        compiler_params=pltpu.CompilerParams(vmem_limit_bytes=2**20),
        cost_estimate=pl.CostEstimate(flops=0, bytes_accessed=4 * jacobian_tiles.size, transcendentals=0),
    )(*far[1:], pltpu.with_memory_space_constraint(tiles, pltpu.HBM))
    coded = pl.pallas_call(
        contribution_kernel,
        out_shape=jax.ShapeDtypeStruct((row_count * (words + 1), TILE), jnp.int32),
        in_specs=[smem] + [vmem] * 5,
        out_specs=vmem,
        scratch_shapes=[
            pltpu.VMEM((2, (own_rows * col_count + 1) * SUB, TILE), F32),
            pltpu.VMEM((row_count * own_rows * SUB, TILE), F32),
            pltpu.SMEM(tile_rows.shape, tile_rows.dtype),
            pltpu.SMEM(tile_cols.shape, tile_cols.dtype),
            pltpu.SemaphoreType.DMA((2,)),
        ],
        compiler_params=pltpu.CompilerParams(vmem_limit_bytes=10 * 2**20),
    )(live_tiles, tile_rows, tile_cols, pair, joined, tiles)
    pieces = coded.reshape(row_count, words + 1, 1, TILE)
    received = lax.all_to_all(pieces, "row", 0, 0, axis_index_groups=[PEERS]).reshape(coded.shape)
    return pl.pallas_call(
        sum_kernel,
        out_shape=jax.ShapeDtypeStruct((own_rows, row_width), F32),
        in_specs=[vmem],
        out_specs=vmem,
        compiler_params=pltpu.CompilerParams(vmem_limit_bytes=4 * 2**20),
    )(received)


def solution(mesh):
    placed = (
        P(("row", "col"), None),
        P(("row", "col"), None, None),
        P(("row", "col")),
        P(("row", "col")),
        P(("row", "col")),
    )
    return jax.shard_map(
        per_device, mesh=mesh, in_specs=placed, out_specs=P(("col", "row"), None), check_vma=False
    )
```

```python
import functools

import jax
import jax.numpy as jnp
from jax import lax
from jax.experimental import pallas as pl
from jax.experimental.pallas import tpu as pltpu
from jax.sharding import PartitionSpec as P

TILE = 128
SUB = 8
GROUP = 48
PEERS = [28, 9, 19, 10, 29, 5, 7, 22, 0, 14, 8, 15, 23, 24, 21, 13, 25, 27, 6, 16, 26, 18, 11, 3, 17, 2, 1, 31, 12, 4, 30, 20]
HOPS = (1, 2, 3)
F32 = jnp.float32


def join_kernel(*refs):
    *part_refs, tiles_ref, out_ref = refs
    for i, part_ref in enumerate(part_refs):
        out_ref[i] = part_ref[...]


def contribution_kernel(live_ref, *refs):
    index_refs, refs = refs[:2], refs[2:]
    pair_ref, joined_ref, tiles_ref, out_ref, x_ref, sum_ref, rows_ref, cols_ref, sems = refs
    copies = [
        pltpu.make_async_copy(source, target, sems.at[i])
        for i, (source, target) in enumerate(zip(index_refs, (rows_ref, cols_ref)))
    ]
    for copy in copies:
        copy.start()
    rows, row_width = pair_ref.shape[0] // 2, pair_ref.shape[1]
    vectors = row_width // TILE
    chips = joined_ref.shape[0] + 1
    words = vectors // 2 * SUB
    pairs = tiles_ref.shape[0]
    blocks = 2 * chips * rows
    me = lax.axis_index("col")
    live = live_ref[0]
    x_ref[...] = jnp.zeros_like(x_ref)
    sum_ref[...] = jnp.zeros_like(sum_ref)
    for hop in range(chips):
        chip = (me // 2) ^ hop
        for part in range(2):
            holder = 2 * chip + lax.rem(me + part, 2)
            base = pl.multiple_of(holder * rows * SUB, rows * SUB)
            for v in range(vectors):
                window = (pl.ds(part * rows, rows), pl.ds(v * TILE, TILE))
                column = pair_ref[window] if hop == 0 else joined_ref[(hop - 1, *window)]
                column = column.astype(F32)
                x_ref[0, pl.ds(base + v, rows, stride=SUB), :] = column
                x_ref[1, pl.ds(base + vectors + v, rows, stride=SUB), :] = column

    for copy in copies:
        copy.wait()

    for step in range(pairs // GROUP):
        products = []
        for k in range(GROUP):
            pair = step * GROUP + k
            halves = []
            for half in range(2):
                slot = 2 * pair + half
                row = jnp.where(slot < live, rows_ref[slot], blocks)
                start = pl.multiple_of(row * SUB, SUB)
                halves.append(x_ref[half, pl.ds(start, SUB), :])
            left = jnp.concatenate(halves, axis=1).astype(jnp.bfloat16)
            products.append(jnp.dot(left, tiles_ref[pair], preferred_element_type=F32))
        for k in range(GROUP):
            pair = step * GROUP + k
            for half in range(2):
                start = pl.multiple_of(cols_ref[2 * pair + half] * SUB, SUB)
                place = pl.ds(start + half * vectors, vectors)
                sum_ref[place, :] += products[k][half * vectors : (half + 1) * vectors, :]

    peers = out_ref.shape[0] // (words + 1)
    own = sum_ref.shape[0] // peers
    for peer in range(peers):
        base, first_row = PEERS[peer] * own, peer * (words + 1)
        totals = []
        for v in range(vectors):
            first = sum_ref[pl.ds(base + v, SUB, stride=SUB), :]
            second = sum_ref[pl.ds(base + vectors + v, SUB, stride=SUB), :]
            totals.append(first + second)
        peaks = functools.reduce(jnp.maximum, [jnp.abs(total) for total in totals])
        peak = jnp.max(peaks, axis=0, keepdims=True)
        power = jnp.ceil(jnp.log2(jnp.maximum(peak, 2.0**-111)) + 0.01)
        scale = jnp.exp2(15.0 - power)
        codes = [jnp.round(total * scale).astype(jnp.int32) for total in totals]
        for half in range(vectors // 2):
            word = (codes[2 * half] << 16) | (codes[2 * half + 1] & 0xFFFF)
            out_ref[first_row + half * SUB : first_row + (half + 1) * SUB, :] = word
        out_ref[first_row + words : first_row + words + 1, :] = power.astype(jnp.int32)


def sum_kernel(in_ref, out_ref):
    vectors = out_ref.shape[1] // TILE
    words = vectors // 2 * SUB
    peers = in_ref.shape[0] // (words + 1)
    totals = [jnp.zeros((SUB, TILE), F32) for _ in range(vectors)]
    for peer in range(peers):
        first_row = peer * (words + 1)
        row = in_ref[first_row + words : first_row + words + 1, :]
        scale = jnp.exp2(row.astype(F32) - 15.0)
        for half in range(vectors // 2):
            word = in_ref[first_row + half * SUB : first_row + (half + 1) * SUB, :]
            totals[2 * half] += (word >> 16).astype(F32) * scale
            totals[2 * half + 1] += ((word << 16) >> 16).astype(F32) * scale
    out_ref[...] = jnp.concatenate(totals, axis=1)


def per_device(krylov, jacobian_tiles, tile_rows, tile_cols, live_tiles):
    col_count = lax.axis_size("col")
    row_count = lax.axis_size("row")
    chips = col_count // 2
    own_rows, row_width = krylov.shape
    slots = jacobian_tiles.shape[0]
    vectors = row_width // TILE
    words = vectors // 2 * SUB
    smem = pl.BlockSpec(memory_space=pltpu.SMEM)
    vmem = pl.BlockSpec(memory_space=pltpu.VMEM)

    other = lax.ppermute(krylov, "col", [(i, i ^ 1) for i in range(col_count)])
    pair = jnp.concatenate([krylov, other])
    far = [None] * chips
    for hop in HOPS:
        steps = [(i, i ^ (2 * hop)) for i in range(col_count)]
        far[hop] = lax.ppermute(pair, "col", steps)
    tiles = jacobian_tiles.reshape(slots // 2, 2 * TILE, TILE)
    joined = pl.pallas_call(
        join_kernel,
        out_shape=jax.ShapeDtypeStruct((chips - 1, 2 * own_rows, row_width), krylov.dtype),
        in_specs=[vmem] * (chips - 1) + [pl.BlockSpec(memory_space=pltpu.HBM)],
        out_specs=vmem,
        compiler_params=pltpu.CompilerParams(vmem_limit_bytes=2**20),
        cost_estimate=pl.CostEstimate(flops=0, bytes_accessed=4 * jacobian_tiles.size, transcendentals=0),
    )(*far[1:], pltpu.with_memory_space_constraint(tiles, pltpu.HBM))
    coded = pl.pallas_call(
        contribution_kernel,
        out_shape=jax.ShapeDtypeStruct((row_count * (words + 1), TILE), jnp.int32),
        in_specs=[smem] + [vmem] * 5,
        out_specs=vmem,
        scratch_shapes=[
            pltpu.VMEM((2, (own_rows * col_count + 1) * SUB, TILE), F32),
            pltpu.VMEM((row_count * own_rows * SUB, TILE), F32),
            pltpu.SMEM(tile_rows.shape, tile_rows.dtype),
            pltpu.SMEM(tile_cols.shape, tile_cols.dtype),
            pltpu.SemaphoreType.DMA((2,)),
        ],
        compiler_params=pltpu.CompilerParams(vmem_limit_bytes=10 * 2**20),
    )(live_tiles, tile_rows, tile_cols, pair, joined, tiles)
    pieces = coded.reshape(row_count, words + 1, 1, TILE)
    received = lax.all_to_all(pieces, "row", 0, 0, axis_index_groups=[PEERS]).reshape(coded.shape)
    return pl.pallas_call(
        sum_kernel,
        out_shape=jax.ShapeDtypeStruct((own_rows, row_width), F32),
        in_specs=[vmem],
        out_specs=vmem,
        compiler_params=pltpu.CompilerParams(vmem_limit_bytes=4 * 2**20),
    )(received)


def solution(mesh):
    placed = (
        P(("row", "col"), None),
        P(("row", "col"), None, None),
        P(("row", "col")),
        P(("row", "col")),
        P(("row", "col")),
    )
    return jax.shard_map(
        per_device, mesh=mesh, in_specs=placed, out_specs=P(("col", "row"), None), check_vma=False
    )
```

```python
import functools

import jax
import jax.numpy as jnp
from jax import lax
from jax.experimental import pallas as pl
from jax.experimental.pallas import tpu as pltpu
from jax.sharding import PartitionSpec as P

TILE = 128
SUB = 8
GROUP = 48
PEERS = [25, 9, 19, 10, 29, 5, 7, 22, 0, 14, 8, 15, 23, 24, 21, 13, 28, 27, 6, 16, 26, 18, 11, 3, 17, 2, 1, 31, 12, 4, 30, 20]
HOPS = (1, 2, 3)
F32 = jnp.float32


def join_kernel(*refs):
    *part_refs, tiles_ref, out_ref = refs
    for i, part_ref in enumerate(part_refs):
        out_ref[i] = part_ref[...]


def contribution_kernel(live_ref, *refs):
    index_refs, refs = refs[:2], refs[2:]
    pair_ref, joined_ref, tiles_ref, out_ref, x_ref, sum_ref, rows_ref, cols_ref, sems = refs
    copies = [
        pltpu.make_async_copy(source, target, sems.at[i])
        for i, (source, target) in enumerate(zip(index_refs, (rows_ref, cols_ref)))
    ]
    for copy in copies:
        copy.start()
    rows, row_width = pair_ref.shape[0] // 2, pair_ref.shape[1]
    vectors = row_width // TILE
    chips = joined_ref.shape[0] + 1
    words = vectors // 2 * SUB
    pairs = tiles_ref.shape[0]
    blocks = 2 * chips * rows
    me = lax.axis_index("col")
    live = live_ref[0]
    x_ref[...] = jnp.zeros_like(x_ref)
    sum_ref[...] = jnp.zeros_like(sum_ref)
    for hop in range(chips):
        chip = (me // 2) ^ hop
        for part in range(2):
            holder = 2 * chip + lax.rem(me + part, 2)
            base = pl.multiple_of(holder * rows * SUB, rows * SUB)
            for v in range(vectors):
                window = (pl.ds(part * rows, rows), pl.ds(v * TILE, TILE))
                column = pair_ref[window] if hop == 0 else joined_ref[(hop - 1, *window)]
                column = column.astype(F32)
                x_ref[0, pl.ds(base + v, rows, stride=SUB), :] = column
                x_ref[1, pl.ds(base + vectors + v, rows, stride=SUB), :] = column

    for copy in copies:
        copy.wait()

    for step in range(pairs // GROUP):
        products = []
        for k in range(GROUP):
            pair = step * GROUP + k
            halves = []
            for half in range(2):
                slot = 2 * pair + half
                row = jnp.where(slot < live, rows_ref[slot], blocks)
                start = pl.multiple_of(row * SUB, SUB)
                halves.append(x_ref[half, pl.ds(start, SUB), :])
            left = jnp.concatenate(halves, axis=1).astype(jnp.bfloat16)
            products.append(jnp.dot(left, tiles_ref[pair], preferred_element_type=F32))
        for k in range(GROUP):
            pair = step * GROUP + k
            for half in range(2):
                start = pl.multiple_of(cols_ref[2 * pair + half] * SUB, SUB)
                place = pl.ds(start + half * vectors, vectors)
                sum_ref[place, :] += products[k][half * vectors : (half + 1) * vectors, :]

    peers = out_ref.shape[0] // (words + 1)
    own = sum_ref.shape[0] // peers
    for peer in range(peers):
        base, first_row = PEERS[peer] * own, peer * (words + 1)
        totals = []
        for v in range(vectors):
            first = sum_ref[pl.ds(base + v, SUB, stride=SUB), :]
            second = sum_ref[pl.ds(base + vectors + v, SUB, stride=SUB), :]
            totals.append(first + second)
        peaks = functools.reduce(jnp.maximum, [jnp.abs(total) for total in totals])
        peak = jnp.max(peaks, axis=0, keepdims=True)
        power = jnp.ceil(jnp.log2(jnp.maximum(peak, 2.0**-111)) + 0.01)
        scale = jnp.exp2(15.0 - power)
        codes = [jnp.round(total * scale).astype(jnp.int32) for total in totals]
        for half in range(vectors // 2):
            word = (codes[2 * half] << 16) | (codes[2 * half + 1] & 0xFFFF)
            out_ref[first_row + half * SUB : first_row + (half + 1) * SUB, :] = word
        out_ref[first_row + words : first_row + words + 1, :] = power.astype(jnp.int32)


def sum_kernel(in_ref, out_ref):
    vectors = out_ref.shape[1] // TILE
    words = vectors // 2 * SUB
    peers = in_ref.shape[0] // (words + 1)
    totals = [jnp.zeros((SUB, TILE), F32) for _ in range(vectors)]
    for peer in range(peers):
        first_row = peer * (words + 1)
        row = in_ref[first_row + words : first_row + words + 1, :]
        scale = jnp.exp2(row.astype(F32) - 15.0)
        for half in range(vectors // 2):
            word = in_ref[first_row + half * SUB : first_row + (half + 1) * SUB, :]
            totals[2 * half] += (word >> 16).astype(F32) * scale
            totals[2 * half + 1] += ((word << 16) >> 16).astype(F32) * scale
    out_ref[...] = jnp.concatenate(totals, axis=1)


def per_device(krylov, jacobian_tiles, tile_rows, tile_cols, live_tiles):
    col_count = lax.axis_size("col")
    row_count = lax.axis_size("row")
    chips = col_count // 2
    own_rows, row_width = krylov.shape
    slots = jacobian_tiles.shape[0]
    vectors = row_width // TILE
    words = vectors // 2 * SUB
    smem = pl.BlockSpec(memory_space=pltpu.SMEM)
    vmem = pl.BlockSpec(memory_space=pltpu.VMEM)

    other = lax.ppermute(krylov, "col", [(i, i ^ 1) for i in range(col_count)])
    pair = jnp.concatenate([krylov, other])
    far = [None] * chips
    for hop in HOPS:
        steps = [(i, i ^ (2 * hop)) for i in range(col_count)]
        far[hop] = lax.ppermute(pair, "col", steps)
    tiles = jacobian_tiles.reshape(slots // 2, 2 * TILE, TILE)
    joined = pl.pallas_call(
        join_kernel,
        out_shape=jax.ShapeDtypeStruct((chips - 1, 2 * own_rows, row_width), krylov.dtype),
        in_specs=[vmem] * (chips - 1) + [pl.BlockSpec(memory_space=pltpu.HBM)],
        out_specs=vmem,
        compiler_params=pltpu.CompilerParams(vmem_limit_bytes=2**20),
        cost_estimate=pl.CostEstimate(flops=0, bytes_accessed=4 * jacobian_tiles.size, transcendentals=0),
    )(*far[1:], pltpu.with_memory_space_constraint(tiles, pltpu.HBM))
    coded = pl.pallas_call(
        contribution_kernel,
        out_shape=jax.ShapeDtypeStruct((row_count * (words + 1), TILE), jnp.int32),
        in_specs=[smem] + [vmem] * 5,
        out_specs=vmem,
        scratch_shapes=[
            pltpu.VMEM((2, (own_rows * col_count + 1) * SUB, TILE), F32),
            pltpu.VMEM((row_count * own_rows * SUB, TILE), F32),
            pltpu.SMEM(tile_rows.shape, tile_rows.dtype),
            pltpu.SMEM(tile_cols.shape, tile_cols.dtype),
            pltpu.SemaphoreType.DMA((2,)),
        ],
        compiler_params=pltpu.CompilerParams(vmem_limit_bytes=10 * 2**20),
    )(live_tiles, tile_rows, tile_cols, pair, joined, tiles)
    pieces = coded.reshape(row_count, words + 1, 1, TILE)
    received = lax.all_to_all(pieces, "row", 0, 0, axis_index_groups=[PEERS]).reshape(coded.shape)
    return pl.pallas_call(
        sum_kernel,
        out_shape=jax.ShapeDtypeStruct((own_rows, row_width), F32),
        in_specs=[vmem],
        out_specs=vmem,
        compiler_params=pltpu.CompilerParams(vmem_limit_bytes=4 * 2**20),
    )(received)


def solution(mesh):
    placed = (
        P(("row", "col"), None),
        P(("row", "col"), None, None),
        P(("row", "col")),
        P(("row", "col")),
        P(("row", "col")),
    )
    return jax.shard_map(
        per_device, mesh=mesh, in_specs=placed, out_specs=P(("col", "row"), None), check_vma=False
    )
```
